256 devices in a mesh: ctx: 32 (over x, z), tp: 8 (over y, core).
Axes of the slice: x: 4, y: 4, z: 8, core: 2. Of those that a mesh axis runs over, the one named last changes fastest.
Arguments:
- queries: bfloat16 [8192, 8192], P('ctx', 'tp'), may hold values from -12 to 12
- keys: bfloat16 [8192, 1024], P('ctx', 'tp'), may hold values from -12 to 12
- values: bfloat16 [8192, 1024], P('ctx', 'tp'), may hold values from -6 to 6
- lengths: int32 [4], replicated, may hold values from 1 to 6144, 8192 in all
- out_weight: bfloat16 [8192, 4096], P('tp'), may hold values from -0.59765625 to 0.59765625
Outputs:
- mixed: bfloat16 [8192, 4096], P('ctx', 'tp')
The draws below stay inside these ranges and needn't reach their ends.
Inputs may be any that keep to these rules, and one draw needn't show every extreme that they name: The 4 lengths sum to 8192; the longest is exactly 6144.
All inputs are finite; a program needn't handle non-finite values.
Results may differ from the reference program's by a relative error of at most 0.014.
Values may be sent and summed in bfloat16 or wider, within the bound.
No kernel may reach another device: no remote copies, remote signals or barrier semaphores. Data moves between devices by JAX's collectives and lax.ppermute only.
A program may use at most 192 MiB of HBM per device.

```python
import math
import jax
import jax.numpy as jnp
import numpy as np
from jax import lax

QH = 64
KVH = 8
HD = 128
FEAT = 4096
TOK_DEV = 256
DOCS = 4
MOST = 6144
PACKED_TOKENS = 8192
N_CTX = 32
N_TP = 8


def paired_draw(key):
    root_random_key = jax.random.fold_in(key, 7)
    random_key_for_query, random_key_for_keys = jax.random.split(root_random_key, 2)
    query_draw = jax.random.truncated_normal(random_key_for_query, -4.0, 4.0, (PACKED_TOKENS, QH * HD), jnp.float32)
    sampled_keys = jax.random.truncated_normal(random_key_for_keys, -4.0, 4.0, (PACKED_TOKENS, KVH * HD), jnp.float32)
    return (query_draw, sampled_keys)


def draw_queries(key, part):
    return paired_draw(key)[0].astype(jnp.bfloat16)


def draw_keys(key, part):
    return paired_draw(key)[1].astype(jnp.bfloat16)


def block_levels(key, shape, shards, least, high):
    loudness, own = 1.0, jax.random.fold_in(key, 6)
    for dim, parts in shards:
        heights = jnp.exp(jax.random.uniform(jax.random.fold_in(own, dim), (parts,), jnp.float32, least / len(shards), high / len(shards)))
        loudness = loudness * jnp.repeat(heights, shape[dim] // parts).reshape([-1 if axis == dim else 1 for axis in range(len(shape))])
    return loudness


def length_profile(count, total, bound, lean):
    portions = [(1 << 20) // math.isqrt(rank ** lean) + 1 for rank in range(2, count + 1)]
    spare, counts = total - bound - (count - 1), [1] * (count - 1)
    while spare > 0:
        movable = [i for i in range(count - 1) if counts[i] < bound]
        mass, budget = sum([portions[i] for i in movable]), spare
        for i in movable:
            more = min(bound - counts[i], max(1, budget * portions[i] // mass), spare)
            counts[i] = counts[i] + more
            spare = spare - more
    return np.array([bound] + counts)


def uneven(stream_key, amount, total, bound, slope):
    if amount == 2:
        one = jax.random.randint(stream_key, (), max(1, total - bound), min(bound, total - 1) + 1)
        return jnp.stack([one, total - one])
    tallies = jnp.asarray(length_profile(amount, total, bound, slope), jnp.int32)
    twos = (amount - 1) // 2
    giver, taker = tallies[1:1 + 2 * twos:2], tallies[2:2 + 2 * twos:2]
    margin = jnp.minimum(giver - 1, bound - taker)
    passed = jax.random.randint(jax.random.fold_in(stream_key, 1), (twos,), 0, 1 << 20) % (margin + 1)
    tallies = tallies.at[1:1 + 2 * twos:2].set(giver - passed).at[2:2 + 2 * twos:2].set(taker + passed)
    return tallies[jax.random.permutation(jax.random.fold_in(stream_key, 2), amount)]


def noise(own_key, dims, deviation, limit, cuts=(), kind=jnp.bfloat16):
    drawn = jax.random.normal(own_key, dims, jnp.float32) * deviation
    if len(cuts) > 0:
        drawn = block_levels(own_key, dims, cuts, -0.22, 0.18) * drawn
    return jnp.clip(drawn, min=-limit, max=limit).astype(kind)


def setup_inputs(seed: int = 0) -> dict:
    seeds = jax.random.split(jax.random.key(seed), 6)
    queries = draw_queries(jax.random.fold_in(seeds[5], 71), 0)
    keys = draw_keys(jax.random.fold_in(seeds[5], 71), 0)
    values = noise(seeds[2], (PACKED_TOKENS, KVH * HD), 1.0, 6.0, ((0, 32), (1, 8)))
    lengths = uneven(seeds[3], DOCS, PACKED_TOKENS, MOST, 2).astype(jnp.int32)
    out_weight = noise(seeds[4], (QH * HD, FEAT), 0.1, 0.59765625, ((0, 8),))
    return {"queries": queries, "keys": keys, "values": values, "lengths": lengths, "out_weight": out_weight}


def row_positions(rows):
    half_rows = TOK_DEV // 2
    device = rows // TOK_DEV
    offset = rows % TOK_DEV
    return jnp.where(offset < half_rows, device * half_rows + offset, (2 * N_CTX - 1 - device) * half_rows + offset - half_rows).astype(jnp.int32)


def position_rows(places):
    half_rows = TOK_DEV // 2
    block_num = places // half_rows
    offset = places % half_rows
    device = jnp.where(block_num < N_CTX, block_num, 2 * N_CTX - 1 - block_num)
    within = jnp.where(block_num < N_CTX, offset, offset + half_rows)
    return (device * TOK_DEV + within).astype(jnp.int32)


def doc_numbers(places, lengths):
    doc_ends = jnp.cumsum(lengths).astype(jnp.int32)
    return jnp.sum((places[:, None] >= doc_ends[None, :]).astype(jnp.int32), axis=1).astype(jnp.int32)


def reference(queries, keys, values, lengths, out_weight):
    group_size = QH // KVH
    score_scale = HD ** -0.5
    block_rows = TOK_DEV
    span_rows = MOST + block_rows
    places = jnp.arange(PACKED_TOKENS, dtype=jnp.int32)
    packed_rows = position_rows(places)
    q_packed = queries[packed_rows]
    k_packed = jnp.concatenate([jnp.zeros((MOST, KVH * HD), keys.dtype), keys[packed_rows]], axis=0)
    v_packed = jnp.concatenate([jnp.zeros((MOST, KVH * HD), values.dtype), values[packed_rows]], axis=0)
    doc_ids = doc_numbers(places, lengths)
    doc_padded = jnp.concatenate([jnp.full((MOST,), -1, jnp.int32), doc_ids])

    def attend_block(block_index):
        first_place = (block_index * block_rows).astype(jnp.int32)
        q_block = lax.dynamic_slice_in_dim(q_packed, first_place, block_rows, 0).reshape(block_rows, KVH, group_size, HD)
        k_block = lax.dynamic_slice_in_dim(k_packed, first_place, span_rows, 0).reshape(span_rows, KVH, HD)
        v_block = lax.dynamic_slice_in_dim(v_packed, first_place, span_rows, 0).reshape(span_rows, KVH, HD)
        q_doc = lax.dynamic_slice_in_dim(doc_ids, first_place, block_rows, 0)
        k_doc = lax.dynamic_slice_in_dim(doc_padded, first_place, span_rows, 0)
        q_place = first_place + jnp.arange(block_rows, dtype=jnp.int32)
        k_place = first_place - MOST + jnp.arange(span_rows, dtype=jnp.int32)
        allowed = (k_doc[None, :] == q_doc[:, None]) & (k_place[None, :] <= q_place[:, None])

        def one_head(number):
            q_head = lax.dynamic_index_in_dim(q_block, number, 1, keepdims=False)
            k_head = lax.dynamic_index_in_dim(k_block, number, 1, keepdims=False)
            v_head = lax.dynamic_index_in_dim(v_block, number, 1, keepdims=False)
            scores = jnp.einsum('tgd,pd->tgp', q_head.astype(jnp.float32), k_head.astype(jnp.float32)) * score_scale
            scores = jnp.where(allowed[:, None, :], scores, -1e30)
            row_max = jnp.max(scores, axis=2, keepdims=True)
            weights = jnp.where(allowed[:, None, :], jnp.exp(scores - row_max), 0.0)
            totals = jnp.sum(weights, axis=2)
            rounded = lax.optimization_barrier(weights.astype(jnp.bfloat16)).astype(jnp.float32)
            summed = jnp.einsum('tgp,pd->tgd', rounded, v_head.astype(jnp.float32))
            return summed / totals[..., None]

        per_head = lax.map(one_head, jnp.arange(KVH, dtype=jnp.int32))
        return jnp.transpose(per_head, (1, 0, 2, 3)).reshape(block_rows, QH * HD).astype(jnp.bfloat16)

    attended = lax.map(attend_block, jnp.arange(PACKED_TOKENS // block_rows, dtype=jnp.int32)).reshape(PACKED_TOKENS, QH * HD)
    attended = attended[row_positions(places)]
    group_rows = QH * HD // N_TP

    def add_group(group, total):
        first = (group * group_rows).astype(jnp.int32)
        part_cols = lax.dynamic_slice_in_dim(attended, first, group_rows, 1)
        part_rows = lax.dynamic_slice_in_dim(out_weight, first, group_rows, 0)
        partial_value = jnp.dot(part_cols, part_rows, preferred_element_type=jnp.float32)
        rounded = lax.optimization_barrier(partial_value.astype(jnp.bfloat16)).astype(jnp.float32)
        return total + rounded

    summed = lax.fori_loop(0, N_TP, add_group, jnp.zeros((PACKED_TOKENS, FEAT), jnp.float32))
    return summed.astype(jnp.bfloat16)
```

```python
import jax
import jax.numpy as jnp
from jax import lax
from jax.experimental import pallas as pl
from jax.experimental.pallas import tpu as pltpu
from jax.sharding import PartitionSpec as P

HD = 128
NX, NZ = 4, 8
NY = 4
CHUNK = 512
XROWS = 96
NEG = -1e30
SCALE2 = (HD ** -0.5) * 1.4426950408889634


def from_x(k):
    return [(((x + k) % NX) * NZ + z, x * NZ + z) for x in range(NX) for z in range(NZ)]


def from_z(k):
    return [(x * NZ + (z + k) % NZ, x * NZ + z) for x in range(NX) for z in range(NZ)]


def from_y(k):
    return [(((y + k) % NY) * 2 + c, y * 2 + c) for y in range(NY) for c in range(2)]


CORES = [(y * 2 + c, y * 2 + 1 - c) for y in range(NY) for c in range(2)]


def ctx(a, perm):
    return lax.ppermute(a, "ctx", perm)


def round_z(a):
    half = a.shape[0] // 2
    up1, up2 = ctx(a, from_z(1)), ctx(a, from_z(2))
    down1, down2 = ctx(a, from_z(-1)), ctx(a, from_z(-2))
    up3, down3 = ctx(up2, from_z(1)), ctx(down2, from_z(-1))
    mid = [ctx(up2[:half], from_z(2)), ctx(down2[half:], from_z(-2))]
    return [a], [up1], [up2], [up3], mid, [down3], [down2], [down1]


def attend_and_project(len_ref, q_ref, w_hbm, *rest):
    narrow, wide = rest[:9], rest[9:13]
    mine_ref, other_ref, kv, w, att, acc, top, kv_sem, w_sem = rest[13:]
    me = lax.axis_index("ctx")
    tp = lax.axis_index("tp")
    mx, mz = me // NZ, me % NZ
    my, mc = tp // 2, tp % 2
    blocks = 2 * NX * NZ
    half = kv.shape[0] // blocks

    def source(kx, kz):
        return ((mx + kx) % NX) * NZ + (mz + kz) % NZ

    def bring(src, start, rows, at):
        pltpu.make_async_copy(
            src.at[pl.ds(start, rows), :],
            kv.at[pl.ds(pl.multiple_of(at, 16), rows), :],
            kv_sem,
        ).start()

    low = half - XROWS
    for kz in range(NZ):
        for kx in range(NX):
            at = source(kx, kz) * half
            if kz < 4:
                bring(narrow[kz], kx * XROWS, XROWS, at)
            elif kz == 4:
                bring(narrow[4 + kx // 2], (kx % 2) * XROWS, XROWS, at)
            else:
                bring(narrow[kz + 1], kx * XROWS, XROWS, at)
            first = kz * (low + half)
            bring(wide[kx], first, low, at + XROWS)
            bring(wide[kx], first + low, half, (blocks - 1) * half - at)
    w_copy = pltpu.make_async_copy(w_hbm, w, w_sem)
    w_copy.start()

    ends = []
    total = 0
    for i in range(4):
        total = total + len_ref[i]
        ends.append(total)

    def begins(p):
        start = jnp.zeros_like(p)
        for e in ends:
            start = jnp.maximum(start, jnp.where(p >= e, e, 0))
        return start

    pltpu.make_async_copy(kv, kv, kv_sem).wait()
    ones = jnp.ones((CHUNK, HD), jnp.bfloat16)

    def rows_of(h, carry):
        block = jnp.where(h == 0, me, blocks - 1 - me)
        q0 = block * half
        last_start = begins(q0 + half - 1)
        acc[...] = jnp.zeros_like(acc)
        top[...] = jnp.full_like(top, NEG)
        q_rows = pl.ds(pl.multiple_of(h * half, half), half)

        def step(j, masked):
            k0 = pl.multiple_of(j * CHUNK, CHUNK)
            k = kv[pl.ds(k0, CHUNK), :HD]
            v = jnp.concatenate([kv[pl.ds(k0, CHUNK), HD:], ones], axis=1)
            if masked:
                kp = k0 + lax.broadcasted_iota(jnp.int32, (half, CHUNK), 1)
                qp = q0 + lax.broadcasted_iota(jnp.int32, (half, CHUNK), 0)
                ok = (kp <= qp) & (kp >= begins(qp))
            for g in range(8):
                rows = slice(g * half, (g + 1) * half)
                s = lax.dot_general(
                    q_ref[q_rows, g * HD : (g + 1) * HD],
                    k,
                    (((1,), (1,)), ((), ())),
                    preferred_element_type=jnp.float32,
                )
                if masked:
                    s = jnp.where(ok, s, NEG)
                old = top[rows, :]
                new = jnp.maximum(old, jnp.max(s, axis=1, keepdims=True))
                p = jnp.exp2((s - jnp.tile(new, (1, CHUNK // HD))) * SCALE2)
                o = jnp.dot(p.astype(jnp.bfloat16), v, preferred_element_type=jnp.float32)
                alpha = jnp.exp2((old - new) * SCALE2)
                acc[rows, :] = acc[rows, :] * jnp.tile(alpha, (1, 2)) + o
                top[rows, :] = new

        def one(j, c):
            whole = (j * CHUNK >= last_start) & (j * CHUNK + CHUNK - 1 <= q0)
            pl.when(whole)(lambda: step(j, False))
            pl.when(jnp.logical_not(whole))(lambda: step(j, True))
            return c

        lax.fori_loop(begins(q0) // CHUNK, (q0 + half - 1) // CHUNK + 1, one, 0)
        for g in range(8):
            rows = slice(g * half, (g + 1) * half)
            att[q_rows, g * HD : (g + 1) * HD] = (acc[rows, :HD] / acc[rows, HD:]).astype(
                jnp.bfloat16
            )
        return carry

    lax.fori_loop(0, 2, rows_of, 0)
    w_copy.wait()
    width = mine_ref.shape[2]
    for k in range(NY):
        for ref, parity in ((mine_ref, mc), (other_ref, 1 - mc)):
            col = pl.multiple_of((((my + k) % NY) * 2 + parity) * width, width)
            ref[k] = jnp.dot(
                att[...], w[:, pl.ds(col, width)], preferred_element_type=jnp.float32
            ).astype(jnp.bfloat16)


def on_device(queries, keys, values, lengths, out_weight):
    tokens = queries.shape[0]
    with jax.named_scope("gather_keys_values"):
        kv = jnp.concatenate([keys, values], axis=1)
        a, b = kv[:XROWS], kv[XROWS:]
        a4 = jnp.concatenate([a] + [ctx(a, from_x(k)) for k in (1, 2, 3)], axis=0)
        narrow = [p for part in round_z(a4) for p in part]
        b8 = jnp.concatenate([p for part in round_z(b) for p in part], axis=0)
        wide = [b8] + [ctx(b8, from_x(k)) for k in (1, 2, 3)]
    any_spec = pl.BlockSpec(memory_space=pl.ANY)
    vmem = pl.BlockSpec(memory_space=pltpu.VMEM)
    width = out_weight.shape[1] // (2 * NY)
    kv_rows = 32 * tokens
    with jax.named_scope("attend_and_project"):
        mine, other = pl.pallas_call(
            attend_and_project,
            out_shape=[jax.ShapeDtypeStruct((NY, tokens, width), jnp.bfloat16)] * 2,
            in_specs=[pl.BlockSpec(memory_space=pltpu.SMEM), vmem] + [any_spec] * 14,
            out_specs=[vmem, vmem],
            scratch_shapes=[
                pltpu.VMEM((kv_rows, 2 * HD), jnp.bfloat16),
                pltpu.VMEM(out_weight.shape, jnp.bfloat16),
                pltpu.VMEM((tokens, queries.shape[1]), jnp.bfloat16),
                pltpu.VMEM((8 * tokens // 2, 2 * HD), jnp.float32),
                pltpu.VMEM((8 * tokens // 2, HD), jnp.float32),
                pltpu.SemaphoreType.DMA,
                pltpu.SemaphoreType.DMA,
            ],
            compiler_params=pltpu.CompilerParams(vmem_limit_bytes=40 * 2**20),
            cost_estimate=pl.CostEstimate(
                flops=6_600_000_000, bytes_accessed=15 * 2**20, transcendentals=9_000_000
            ),
        )(lengths, queries, out_weight, *narrow, *wide)
    with jax.named_scope("sum_over_heads"):
        theirs = lax.ppermute(other, "tp", CORES)

        def pair(k):
            return (mine[k].astype(jnp.float32) + theirs[k].astype(jnp.float32)).astype(jnp.bfloat16)

        out = mine[0].astype(jnp.float32) + theirs[0].astype(jnp.float32)
        for k in (1, 2, 3):
            out = out + lax.ppermute(pair(k), "tp", from_y(-k)).astype(jnp.float32)
        return out.astype(jnp.bfloat16)


def solution(mesh):
    return jax.shard_map(
        on_device,
        mesh=mesh,
        in_specs=(P("ctx", "tp"), P("ctx", "tp"), P("ctx", "tp"), P(), P("tp", None)),
        out_specs=P("ctx", "tp"),
        check_vma=False,
    )
```

```python
import functools

import jax
import jax.numpy as jnp
from jax import lax
from jax.experimental import pallas as pl
from jax.experimental.pallas import tpu as pltpu
from jax.sharding import PartitionSpec as P

HD = 128
GROUP = 8
NX, NZ, NY = 4, 8, 4
HALF = 128
BLOCKS = 2 * NX * NZ
CHUNK = 512
NEG = -1e30
SCALE2 = (HD ** -0.5) * 1.4426950408889634
FIRST_Z, LATER_Z = (0, 1, 7, 2), (6, 3, 4, 5)
VMEM = pl.BlockSpec(memory_space=pltpu.VMEM)
ANY = pl.BlockSpec(memory_space=pl.ANY)


def from_x(k):
    return [(((x + k) % NX) * NZ + z, x * NZ + z) for x in range(NX) for z in range(NZ)]


def from_z(k):
    return [(x * NZ + (z + k) % NZ, x * NZ + z) for x in range(NX) for z in range(NZ)]


def from_y(k):
    return [(((y + k) % NY) * 2 + c, y * 2 + c) for y in range(NY) for c in range(2)]


CORES = [(y * 2 + c, y * 2 + 1 - c) for y in range(NY) for c in range(2)]


def ctx(a, perm):
    return lax.ppermute(a, "ctx", perm)


def lay_beside(k_ref, v_ref, out):
    out[:, :HD] = k_ref[...]
    out[:, HD:] = v_ref[...]


def lay_together(*refs):
    at = 0
    for piece in refs[:-1]:
        refs[-1][at : at + piece.shape[0], :] = piece[...]
        at += piece.shape[0]


def together(parts):
    rows = sum(p.shape[0] for p in parts)
    return pl.pallas_call(
        lay_together,
        out_shape=jax.ShapeDtypeStruct((rows, parts[0].shape[1]), parts[0].dtype),
        in_specs=[VMEM] * len(parts),
        out_specs=VMEM,
        compiler_params=pltpu.CompilerParams(vmem_limit_bytes=8 * 2**20),
    )(*parts)


def attend(rows, first, last, *refs):
    refs = list(refs)
    take = lambda n: [refs.pop(0) for _ in range(n)]
    len_hbm, q_hbm = take(2)
    w_hbm = take(1)[0] if last else None
    pieces = take(2 * len(rows))
    state = [] if first else take(2)
    mine_ref, other_ref = take(2) if last else (None, None)
    acc, top, kv, q, lens, kv_sem, q_sem, len_sem = take(8)
    me = lax.axis_index("ctx")
    mx, mz = me // NZ, me % NZ
    span = NZ * HALF

    len_copy = pltpu.make_async_copy(len_hbm, lens, len_sem)
    len_copy.start()
    q_copy = pltpu.make_async_copy(q_hbm, q, q_sem)
    q_copy.start()
    for r in range(len(rows)):
        for ref, offsets in zip(pieces[2 * r : 2 * r + 2], (FIRST_Z, LATER_Z)):
            for i, kz in enumerate(offsets):
                z = (mz + kz) % NZ
                for part, at in ((0, z), (1, 2 * NZ - 1 - z)):
                    pltpu.make_async_copy(
                        ref.at[pl.ds((2 * i + part) * HALF, HALF), :],
                        kv.at[pl.ds(pl.multiple_of((2 * r * NZ + at) * HALF, HALF), HALF), :],
                        kv_sem,
                    ).start()
    if last:
        w, att, w_sem = take(3)
        w_copy = pltpu.make_async_copy(w_hbm, w, w_sem)
        w_copy.start()
    if first:
        acc[...] = jnp.zeros_like(acc)
        top[...] = jnp.full_like(top, NEG)
    else:
        acc[...] = state[0][...]
        top[...] = state[1][...]
    len_copy.wait()
    ends = []
    total = 0
    for i in range(4):
        total = total + lens[i]
        ends.append(total)

    def begins(p):
        start = jnp.zeros_like(p)
        for e in ends:
            start = jnp.maximum(start, jnp.where(p >= e, e, 0))
        return start

    q_copy.wait()
    pltpu.make_async_copy(kv, kv, kv_sem).wait()
    ones = jnp.ones((CHUNK, HD), jnp.bfloat16)
    per = span // CHUNK

    def rows_of(h, carry):
        q0 = jnp.where(h == 0, me, BLOCKS - 1 - me) * HALF
        first_start, last_start = begins(q0), begins(q0 + HALF - 1)
        q_rows = pl.ds(pl.multiple_of(h * HALF, HALF), HALF)

        def step(c, k0, masked):
            s0 = pl.multiple_of(c * CHUNK, CHUNK)
            k = kv[pl.ds(s0, CHUNK), :HD]
            v = jnp.concatenate([kv[pl.ds(s0, CHUNK), HD:], ones], axis=1)
            if masked:
                kp = k0 + lax.broadcasted_iota(jnp.int32, (HALF, CHUNK), 1)
                qp = q0 + lax.broadcasted_iota(jnp.int32, (HALF, CHUNK), 0)
                ok = (kp <= qp) & (kp >= begins(qp))
            for g in range(GROUP):
                at = slice(g * HALF, (g + 1) * HALF)
                s = lax.dot_general(
                    q[q_rows, g * HD : (g + 1) * HD],
                    k,
                    (((1,), (1,)), ((), ())),
                    preferred_element_type=jnp.float32,
                )
                if masked:
                    s = jnp.where(ok, s, NEG)
                old = top[h, at, :]
                new = jnp.maximum(old, jnp.max(s, axis=1, keepdims=True))
                p = jnp.exp2((s - jnp.tile(new, (1, CHUNK // HD))) * SCALE2)
                o = jnp.dot(p.astype(jnp.bfloat16), v, preferred_element_type=jnp.float32)
                alpha = jnp.exp2((old - new) * SCALE2)
                acc[h, at, :] = acc[h, at, :] * jnp.tile(alpha, (1, 2)) + o
                top[h, at, :] = new

        def one(c, carry):
            r, late, j = c // (2 * per), (c // per) % 2, c % per
            kx = rows[0]
            for i in range(1, len(rows)):
                kx = jnp.where(r == i, rows[i], kx)
            x = (mx + kx) % NX
            k0 = jnp.where(late == 0, x, 2 * NX - 1 - x) * span + j * CHUNK
            some = (k0 <= q0 + HALF - 1) & (k0 + CHUNK - 1 >= first_start)
            whole = (k0 >= last_start) & (k0 + CHUNK - 1 <= q0)
            pl.when(whole)(lambda: step(c, k0, False))
            pl.when(some & jnp.logical_not(whole))(lambda: step(c, k0, True))
            return carry

        lax.fori_loop(0, len(rows) * 2 * per, one, 0)
        if last:
            for g in range(GROUP):
                at = slice(g * HALF, (g + 1) * HALF)
                att[q_rows, g * HD : (g + 1) * HD] = (
                    acc[h, at, :HD] / acc[h, at, HD:]
                ).astype(jnp.bfloat16)
        return carry

    lax.fori_loop(0, 2, rows_of, 0)
    if last:
        w_copy.wait()
        tp = lax.axis_index("tp")
        my, mc = tp // 2, tp % 2
        width = mine_ref.shape[2]
        for k in range(NY):
            for ref, parity in ((mine_ref, mc), (other_ref, 1 - mc)):
                col = pl.multiple_of((((my + k) % NY) * 2 + parity) * width, width)
                ref[k] = jnp.dot(
                    att[...], w[:, pl.ds(col, width)], preferred_element_type=jnp.float32
                ).astype(jnp.bfloat16)


def attend_to(rows, lengths, queries, pieces, state=None, out_weight=None):
    first, last = state is None, out_weight is not None
    tokens = queries.shape[0]
    state_shape = [(2, GROUP * HALF, 2 * HD), (2, GROUP * HALF, HD)]
    outs = [jax.ShapeDtypeStruct(s, jnp.float32) for s in state_shape]
    operands = [lengths, queries] + ([out_weight] if last else []) + pieces
    specs = [ANY] * len(operands) + ([] if first else [VMEM] * 2)
    operands = operands + ([] if first else list(state))
    scratch = [
        pltpu.VMEM((len(rows) * 2 * NZ * HALF, 2 * HD), jnp.bfloat16),
        pltpu.VMEM(queries.shape, jnp.bfloat16),
        pltpu.SMEM(lengths.shape, jnp.int32),
    ] + [pltpu.SemaphoreType.DMA] * 3
    flops = 1_100_000_000 * len(rows)
    if last:
        width = out_weight.shape[1] // (2 * NY)
        scratch = [pltpu.VMEM(s, jnp.float32) for s in state_shape] + scratch
        scratch += [
            pltpu.VMEM(out_weight.shape, jnp.bfloat16),
            pltpu.VMEM(queries.shape, jnp.bfloat16),
            pltpu.SemaphoreType.DMA,
        ]
        outs = [jax.ShapeDtypeStruct((NY, tokens, width), jnp.bfloat16)] * 2
        flops += 2_150_000_000
    return pl.pallas_call(
        functools.partial(attend, rows, first, last),
        out_shape=outs,
        in_specs=specs,
        out_specs=[VMEM] * 2,
        scratch_shapes=scratch,
        compiler_params=pltpu.CompilerParams(vmem_limit_bytes=(36 if last else 20) * 2**20),
        cost_estimate=pl.CostEstimate(
            flops=flops, bytes_accessed=6 * 2**20, transcendentals=3_000_000 * len(rows)
        ),
    )(*operands)


def on_device(queries, keys, values, lengths, out_weight):
    tokens = queries.shape[0]
    with jax.named_scope("gather_keys_values"):
        kv = pl.pallas_call(
            lay_beside,
            out_shape=jax.ShapeDtypeStruct((tokens, 2 * HD), keys.dtype),
            in_specs=[VMEM] * 2,
            out_specs=VMEM,
        )(keys, values)
        up2, down2 = ctx(kv, from_z(2)), ctx(kv, from_z(-2))
        up1, down1 = ctx(kv, from_z(1)), ctx(kv, from_z(-1))
        early = together([kv, up1, down1, up2])
        right_a, left_a = ctx(early, from_x(1)), ctx(early, from_x(-1))
        up3, down3 = ctx(up2, from_z(1)), ctx(down2, from_z(-1))
        up4 = ctx(up2, from_z(2))
        later = together([down2, up3, up4, down3])
        right_b, left_b = ctx(later, from_x(1)), ctx(later, from_x(-1))
        far_a = ctx(right_a, from_x(1))
        far_b = ctx(left_b, from_x(-1))
    with jax.named_scope("attend_own_row"):
        state = attend_to((0,), lengths, queries, [early, later])
    with jax.named_scope("attend_next_rows"):
        state = attend_to((1, 3), lengths, queries, [right_a, right_b, left_a, left_b], state)
    with jax.named_scope("attend_far_row_and_project"):
        mine, other = attend_to((2,), lengths, queries, [far_a, far_b], state, out_weight)
    with jax.named_scope("sum_over_heads"):
        theirs = lax.ppermute(other, "tp", CORES)

        def pair(k):
            return (mine[k].astype(jnp.float32) + theirs[k].astype(jnp.float32)).astype(jnp.bfloat16)

        out = mine[0].astype(jnp.float32) + theirs[0].astype(jnp.float32)
        for k in (2, 1, 3):
            out = out + lax.ppermute(pair(k), "tp", from_y(-k)).astype(jnp.float32)
        return out.astype(jnp.bfloat16)


def solution(mesh):
    return jax.shard_map(
        on_device,
        mesh=mesh,
        in_specs=(P("ctx", "tp"), P("ctx", "tp"), P("ctx", "tp"), P(), P("tp", None)),
        out_specs=P("ctx", "tp"),
        check_vma=False,
    )
```

```python
import functools

import jax
import jax.numpy as jnp
from jax import lax
from jax.experimental import pallas as pl
from jax.experimental.pallas import tpu as pltpu
from jax.sharding import PartitionSpec as P

HD = 128
GROUP = 8
NX, NZ, NY = 4, 8, 4
HALF = 128
BLOCKS = 2 * NX * NZ
NEG = -1e30
SCALE2 = (HD ** -0.5) * 1.4426950408889634
FIRST_Z, LATER_Z = (0, 1, 7, 2, 6), (3, 4, 5)
VMEM = pl.BlockSpec(memory_space=pltpu.VMEM)
ANY = pl.BlockSpec(memory_space=pl.ANY)


def from_x(k):
    return [(((x + k) % NX) * NZ + z, x * NZ + z) for x in range(NX) for z in range(NZ)]


def from_z(k):
    return [(x * NZ + (z + k) % NZ, x * NZ + z) for x in range(NX) for z in range(NZ)]


def from_y(k):
    return [(((y + k) % NY) * 2 + c, y * 2 + c) for y in range(NY) for c in range(2)]


OVER = [(x * NZ + (z + (2 if z % 2 == 0 else -2)) % NZ, x * NZ + z) for x in range(NX) for z in range(NZ)]
CORES = [(y * 2 + c, y * 2 + 1 - c) for y in range(NY) for c in range(2)]


def ctx(a, perm):
    return lax.ppermute(a, "ctx", perm)


def lay_beside(k_hbm, v_hbm, out, k_sem, v_sem):
    copies = [
        pltpu.make_async_copy(k_hbm, out.at[:, pl.ds(0, HD)], k_sem),
        pltpu.make_async_copy(v_hbm, out.at[:, pl.ds(HD, HD)], v_sem),
    ]
    for copy in copies:
        copy.start()
    for copy in copies:
        copy.wait()


def lay_together(*refs):
    at = 0
    for piece in refs[:-1]:
        refs[-1][at : at + piece.shape[0], :] = piece[...]
        at += piece.shape[0]


def together(parts):
    rows = sum(p.shape[0] for p in parts)
    return pl.pallas_call(
        lay_together,
        out_shape=jax.ShapeDtypeStruct((rows, parts[0].shape[1]), parts[0].dtype),
        in_specs=[VMEM] * len(parts),
        out_specs=VMEM,
        compiler_params=pltpu.CompilerParams(vmem_limit_bytes=8 * 2**20),
    )(*parts)


def attend(rows, first, last, *refs):
    refs = list(refs)
    take = lambda n: [refs.pop(0) for _ in range(n)]
    len_hbm, q = take(2)
    w_hbm = take(1)[0] if last else None
    pieces = take(2 * len(rows))
    state = [] if first else take(2)
    mine_ref, other_ref = take(2) if last else (None, None)
    acc, top, lens, len_sem = take(4)
    me = lax.axis_index("ctx")
    mx, mz = me // NZ, me % NZ
    span = NZ * HALF

    len_copy = pltpu.make_async_copy(len_hbm, lens, len_sem)
    len_copy.start()
    if last:
        att, w, w_sem = take(3)
        w_copy = pltpu.make_async_copy(w_hbm, w, w_sem)
        w_copy.start()
    if first:
        acc[...] = jnp.zeros_like(acc)
        top[...] = jnp.full_like(top, NEG)
    else:
        acc[...] = state[0][...]
        top[...] = state[1][...]
    len_copy.wait()
    ends = []
    total = 0
    for i in range(4):
        total = total + lens[i]
        ends.append(total)

    def begins(p):
        start = jnp.zeros_like(p)
        for e in ends:
            start = jnp.maximum(start, jnp.where(p >= e, e, 0))
        return start

    ones = jnp.ones((span, HD), jnp.bfloat16)

    def step(blocks, h, q0, late, k0, masked):
        k, v, kp = [], [], []
        for ref, i, kz in blocks:
            at = pl.ds(pl.multiple_of((2 * i + late) * HALF, HALF), HALF)
            k.append(ref[at, :HD])
            v.append(ref[at, HD:])
            z = (mz + kz) % NZ
            if masked:
                base = k0 + jnp.where(late == 0, z, NZ - 1 - z) * HALF
                kp.append(base + lax.broadcasted_iota(jnp.int32, (HALF, HALF), 1))
        k = jnp.concatenate(k, axis=0)
        v = jnp.concatenate([jnp.concatenate(v, axis=0), ones], axis=1)
        if masked:
            kp = jnp.concatenate(kp, axis=1)
            qp = q0 + lax.broadcasted_iota(jnp.int32, (HALF, HD), 0)
            begin = jnp.tile(begins(qp), (1, NZ))
            ok = (kp <= jnp.tile(qp, (1, NZ))) & (kp >= begin)
        q_rows = pl.ds(pl.multiple_of(h * HALF, HALF), HALF)
        for g in range(GROUP):
            at = slice(g * HALF, (g + 1) * HALF)
            s = lax.dot_general(
                q[q_rows, g * HD : (g + 1) * HD],
                k,
                (((1,), (1,)), ((), ())),
                preferred_element_type=jnp.float32,
            )
            if masked:
                s = jnp.where(ok, s, NEG)
            old = top[h, at, :]
            new = jnp.maximum(old, jnp.max(s, axis=1, keepdims=True))
            p = jnp.exp2((s - jnp.tile(new, (1, NZ))) * SCALE2)
            o = jnp.dot(p.astype(jnp.bfloat16), v, preferred_element_type=jnp.float32)
            alpha = jnp.exp2((old - new) * SCALE2)
            acc[h, at, :] = acc[h, at, :] * jnp.tile(alpha, (1, 2)) + o
            top[h, at, :] = new

    for r, kx in enumerate(rows):
        x = (mx + kx) % NX
        blocks = [
            (ref, i, kz)
            for ref, offsets in zip(pieces[2 * r : 2 * r + 2], (FIRST_Z, LATER_Z))
            for i, kz in enumerate(offsets)
        ]

        def one(n, carry, x=x, blocks=blocks):
            h, late = jnp.where(n == 0, 0, 1), jnp.where(n == 2, 1, 0)
            q0 = jnp.where(h == 0, me, BLOCKS - 1 - me) * HALF
            first_start, last_start = begins(q0), begins(q0 + HALF - 1)
            k0 = jnp.where(late == 0, x, 2 * NX - 1 - x) * span
            some = (k0 <= q0 + HALF - 1) & (k0 + span - 1 >= first_start)
            whole = (k0 >= last_start) & (k0 + span - 1 <= q0)
            pl.when(whole)(lambda: step(blocks, h, q0, late, k0, False))
            pl.when(some & jnp.logical_not(whole))(lambda: step(blocks, h, q0, late, k0, True))
            return carry

        lax.fori_loop(0, 3, one, 0)

    if last:
        for h in range(2):
            for g in range(GROUP):
                at = slice(g * HALF, (g + 1) * HALF)
                att[h * HALF : (h + 1) * HALF, g * HD : (g + 1) * HD] = (
                    acc[h, at, :HD] / acc[h, at, HD:]
                ).astype(jnp.bfloat16)
        w_copy.wait()
        tp = lax.axis_index("tp")
        my, mc = tp // 2, tp % 2
        width = mine_ref.shape[2]
        for k in range(NY):
            for ref, parity in ((mine_ref, mc), (other_ref, 1 - mc)):
                col = pl.multiple_of((((my + k) % NY) * 2 + parity) * width, width)
                ref[k] = jnp.dot(
                    att[...], w[:, pl.ds(col, width)], preferred_element_type=jnp.float32
                ).astype(jnp.bfloat16)


def attend_to(rows, lengths, queries, pieces, state=None, out_weight=None):
    first, last = state is None, out_weight is not None
    tokens = queries.shape[0]
    state_shape = [(2, GROUP * HALF, 2 * HD), (2, GROUP * HALF, HD)]
    outs = [jax.ShapeDtypeStruct(s, jnp.float32) for s in state_shape]
    operands = [lengths, queries] + ([out_weight] if last else []) + pieces
    operands += [] if first else list(state)
    scratch = [pltpu.SMEM(lengths.shape, jnp.int32), pltpu.SemaphoreType.DMA]
    flops = 1_100_000_000 * len(rows)
    if last:
        width = out_weight.shape[1] // (2 * NY)
        scratch = [pltpu.VMEM(s, jnp.float32) for s in state_shape] + scratch
        scratch += [
            pltpu.VMEM(queries.shape, jnp.bfloat16),
            pltpu.VMEM(out_weight.shape, jnp.bfloat16),
            pltpu.SemaphoreType.DMA,
        ]
        outs = [jax.ShapeDtypeStruct((NY, tokens, width), jnp.bfloat16)] * 2
        flops += 2_150_000_000
    return pl.pallas_call(
        functools.partial(attend, rows, first, last),
        out_shape=outs,
        in_specs=[ANY, VMEM] + ([ANY] if last else []) + [VMEM] * (len(operands) - 2 - last),
        out_specs=[VMEM] * 2,
        scratch_shapes=scratch,
        compiler_params=pltpu.CompilerParams(vmem_limit_bytes=(22 if last else 14) * 2**20),
        cost_estimate=pl.CostEstimate(
            flops=flops, bytes_accessed=6 * 2**20, transcendentals=3_000_000 * len(rows)
        ),
    )(*operands)


def on_device(queries, keys, values, lengths, out_weight):
    tokens = queries.shape[0]
    with jax.named_scope("gather_keys_values"):
        kv = pl.pallas_call(
            lay_beside,
            out_shape=jax.ShapeDtypeStruct((tokens, 2 * HD), keys.dtype),
            in_specs=[ANY] * 2,
            out_specs=VMEM,
            scratch_shapes=[pltpu.SemaphoreType.DMA] * 2,
            compiler_params=pltpu.CompilerParams(vmem_limit_bytes=2 * 2**20),
        )(keys, values)
        up2, down2 = ctx(kv, from_z(2)), ctx(kv, from_z(-2))
        up1, down1 = ctx(kv, from_z(1)), ctx(kv, from_z(-1))
        early = together([kv, up1, down1, up2, down2])
        right_a, left_a = ctx(early, from_x(1)), ctx(early, from_x(-1))
        up3, down3 = ctx(up2, from_z(1)), ctx(down2, from_z(-1))
        even = lax.axis_index("ctx") % 2 == 0
        over = ctx(jnp.where(even, up2, down2), OVER)
        later = together([up3, over, down3])
        right_b, left_b = ctx(later, from_x(1)), ctx(later, from_x(-1))
    with jax.named_scope("attend_own_row"):
        state = attend_to((0,), lengths, queries, [early, later])
    with jax.named_scope("gather_keys_values"):
        right_a, left_a = lax.optimization_barrier((right_a, left_a))
        far_a = ctx(right_a, from_x(1))
        right_b, left_b, state = lax.optimization_barrier((right_b, left_b, state))
        far_b = ctx(left_b, from_x(-1))
    with jax.named_scope("attend_next_rows"):
        state = attend_to((1, 3), lengths, queries, [right_a, right_b, left_a, left_b], state)
    with jax.named_scope("attend_far_row_and_project"):
        mine, other = attend_to((2,), lengths, queries, [far_a, far_b], state, out_weight)
    with jax.named_scope("sum_over_heads"):
        theirs = lax.ppermute(other, "tp", CORES)

        def pair(k):
            return (mine[k].astype(jnp.float32) + theirs[k].astype(jnp.float32)).astype(jnp.bfloat16)

        out = mine[0].astype(jnp.float32) + theirs[0].astype(jnp.float32)
        for k in (2, 1, 3):
            out = out + lax.ppermute(pair(k), "tp", from_y(-k)).astype(jnp.float32)
        return out.astype(jnp.bfloat16)


def solution(mesh):
    return jax.shard_map(
        on_device,
        mesh=mesh,
        in_specs=(P("ctx", "tp"), P("ctx", "tp"), P("ctx", "tp"), P(), P("tp", None)),
        out_specs=P("ctx", "tp"),
        check_vma=False,
    )
```

```python
import functools

import jax
import jax.numpy as jnp
from jax import lax
from jax.experimental import pallas as pl
from jax.experimental.pallas import tpu as pltpu
from jax.sharding import PartitionSpec as P

HD = 128
GROUP = 8
NX, NZ, NY = 4, 8, 4
HALF = 128
BLOCKS = 2 * NX * NZ
NEG = -1e30
SCALE2 = (HD ** -0.5) * 1.4426950408889634
FIRST_Z, LATER_Z = (0, 1, 7, 2, 6), (3, 4, 5)
VMEM = pl.BlockSpec(memory_space=pltpu.VMEM)
ANY = pl.BlockSpec(memory_space=pl.ANY)


def from_x(k):
    return [(((x + k) % NX) * NZ + z, x * NZ + z) for x in range(NX) for z in range(NZ)]


def from_z(k):
    return [(x * NZ + (z + k) % NZ, x * NZ + z) for x in range(NX) for z in range(NZ)]


def from_y(k):
    return [(((y + k) % NY) * 2 + c, y * 2 + c) for y in range(NY) for c in range(2)]


OVER = [(x * NZ + (z + (2 if z % 2 == 0 else -2)) % NZ, x * NZ + z) for x in range(NX) for z in range(NZ)]
CORES = [(y * 2 + c, y * 2 + 1 - c) for y in range(NY) for c in range(2)]


def ctx(a, perm):
    return lax.ppermute(a, "ctx", perm)


def lay_together(*refs):
    at = 0
    for piece in refs[:-1]:
        refs[-1][at : at + piece.shape[0], :] = piece[...]
        at += piece.shape[0]


def together(parts):
    rows = sum(p.shape[0] for p in parts)
    return pl.pallas_call(
        lay_together,
        out_shape=jax.ShapeDtypeStruct((rows, parts[0].shape[1]), parts[0].dtype),
        in_specs=[VMEM] * len(parts),
        out_specs=VMEM,
        compiler_params=pltpu.CompilerParams(vmem_limit_bytes=8 * 2**20),
    )(*parts)


def attend(rows, first, last, *refs):
    refs = list(refs)
    take = lambda n: [refs.pop(0) for _ in range(n)]
    len_hbm, q = take(2)
    w = take(1)[0] if last else None
    pieces = take(2 * len(rows))
    state = [] if first else take(2)
    att, mine_ref, other_ref = take(3) if last else (None, None, None)
    acc, top, lens, len_sem = take(4)
    me = lax.axis_index("ctx")
    mx, mz = me // NZ, me % NZ
    span = NZ * HALF

    len_copy = pltpu.make_async_copy(len_hbm, lens, len_sem)
    len_copy.start()
    if first:
        acc[...] = jnp.zeros_like(acc)
        top[...] = jnp.full_like(top, NEG)
    else:
        acc[...] = state[0][...]
        top[...] = state[1][...]
    len_copy.wait()
    ends = []
    total = 0
    for i in range(4):
        total = total + lens[i]
        ends.append(total)

    def begins(p):
        start = jnp.zeros_like(p)
        for e in ends:
            start = jnp.maximum(start, jnp.where(p >= e, e, 0))
        return start

    ones = jnp.ones((span, HD), jnp.bfloat16)

    def step(blocks, h, q0, late, k0, masked):
        k, v, kp = [], [], []
        for ref, i, kz in blocks:
            at = pl.ds(pl.multiple_of((2 * i + late) * HALF, HALF), HALF)
            k.append(ref[at, :HD])
            v.append(ref[at, HD:])
            z = (mz + kz) % NZ
            if masked:
                base = k0 + jnp.where(late == 0, z, NZ - 1 - z) * HALF
                kp.append(base + lax.broadcasted_iota(jnp.int32, (HALF, HALF), 1))
        k = jnp.concatenate(k, axis=0)
        v = jnp.concatenate([jnp.concatenate(v, axis=0), ones], axis=1)
        if masked:
            kp = jnp.concatenate(kp, axis=1)
            qp = q0 + lax.broadcasted_iota(jnp.int32, (HALF, HD), 0)
            begin = jnp.tile(begins(qp), (1, NZ))
            ok = (kp <= jnp.tile(qp, (1, NZ))) & (kp >= begin)
        q_rows = pl.ds(pl.multiple_of(h * HALF, HALF), HALF)
        for g in range(GROUP):
            at = slice(g * HALF, (g + 1) * HALF)
            s = lax.dot_general(
                q[q_rows, g * HD : (g + 1) * HD],
                k,
                (((1,), (1,)), ((), ())),
                preferred_element_type=jnp.float32,
            )
            if masked:
                s = jnp.where(ok, s, NEG)
            old = top[h, at, :]
            new = jnp.maximum(old, jnp.max(s, axis=1, keepdims=True))
            p = jnp.exp2((s - jnp.tile(new, (1, NZ))) * SCALE2)
            o = jnp.dot(p.astype(jnp.bfloat16), v, preferred_element_type=jnp.float32)
            alpha = jnp.exp2((old - new) * SCALE2)
            acc[h, at, :] = acc[h, at, :] * jnp.tile(alpha, (1, 2)) + o
            top[h, at, :] = new

    for r, kx in enumerate(rows):
        x = (mx + kx) % NX
        blocks = [
            (ref, i, kz)
            for ref, offsets in zip(pieces[2 * r : 2 * r + 2], (FIRST_Z, LATER_Z))
            for i, kz in enumerate(offsets)
        ]

        def one(n, carry, x=x, blocks=blocks):
            h, late = jnp.where(n == 0, 0, 1), jnp.where(n == 2, 1, 0)
            q0 = jnp.where(h == 0, me, BLOCKS - 1 - me) * HALF
            first_start, last_start = begins(q0), begins(q0 + HALF - 1)
            k0 = jnp.where(late == 0, x, 2 * NX - 1 - x) * span
            some = (k0 <= q0 + HALF - 1) & (k0 + span - 1 >= first_start)
            whole = (k0 >= last_start) & (k0 + span - 1 <= q0)
            pl.when(whole)(lambda: step(blocks, h, q0, late, k0, False))
            pl.when(some & jnp.logical_not(whole))(lambda: step(blocks, h, q0, late, k0, True))
            return carry

        lax.fori_loop(0, 3, one, 0)

    if last:
        for h in range(2):
            for g in range(GROUP):
                at = slice(g * HALF, (g + 1) * HALF)
                att[h * HALF : (h + 1) * HALF, g * HD : (g + 1) * HD] = (
                    acc[h, at, :HD] / acc[h, at, HD:]
                ).astype(jnp.bfloat16)
        for ref, same in ((other_ref, False), (mine_ref, True)):
            ref[...] = projected(att, w, 2, same)


def projected(att, w, k, same):
    tp = lax.axis_index("tp")
    width = w.shape[1] // (2 * NY)
    core = tp % 2 if same else 1 - tp % 2
    col = pl.multiple_of((((tp // 2 + k) % NY) * 2 + core) * width, width)
    return jnp.dot(
        att[...], w[:, pl.ds(col, width)], preferred_element_type=jnp.float32
    ).astype(jnp.bfloat16)


def project(ks, same, att, w, out):
    for i, k in enumerate(ks):
        out[i] = projected(att, w, k, same)


def project_to(ks, same, att, out_weight):
    shape = (len(ks), att.shape[0], out_weight.shape[1] // (2 * NY))
    return pl.pallas_call(
        functools.partial(project, ks, same),
        out_shape=jax.ShapeDtypeStruct(shape, jnp.bfloat16),
        in_specs=[VMEM] * 2,
        out_specs=VMEM,
        compiler_params=pltpu.CompilerParams(vmem_limit_bytes=14 * 2**20),
        cost_estimate=pl.CostEstimate(
            flops=270_000_000 * len(ks), bytes_accessed=2**20, transcendentals=0
        ),
    )(att, out_weight)


def attend_to(rows, lengths, queries, pieces, state=None, out_weight=None):
    first, last = state is None, out_weight is not None
    tokens = queries.shape[0]
    state_shape = [(2, GROUP * HALF, 2 * HD), (2, GROUP * HALF, HD)]
    outs = [jax.ShapeDtypeStruct(s, jnp.float32) for s in state_shape]
    operands = [lengths, queries] + ([out_weight] if last else []) + pieces
    operands += [] if first else list(state)
    scratch = [pltpu.SMEM(lengths.shape, jnp.int32), pltpu.SemaphoreType.DMA]
    flops = 1_100_000_000 * len(rows)
    if last:
        width = out_weight.shape[1] // (2 * NY)
        scratch = [pltpu.VMEM(s, jnp.float32) for s in state_shape] + scratch
        outs = [jax.ShapeDtypeStruct(queries.shape, jnp.bfloat16)]
        outs += [jax.ShapeDtypeStruct((tokens, width), jnp.bfloat16)] * 2
        flops += 540_000_000
    return pl.pallas_call(
        functools.partial(attend, rows, first, last),
        out_shape=outs,
        in_specs=[ANY] + [VMEM] * (len(operands) - 1),
        out_specs=[VMEM] * len(outs),
        scratch_shapes=scratch,
        compiler_params=pltpu.CompilerParams(vmem_limit_bytes=(22 if last else 14) * 2**20),
        cost_estimate=pl.CostEstimate(
            flops=flops, bytes_accessed=6 * 2**20, transcendentals=3_000_000 * len(rows)
        ),
    )(*operands)


def on_device(queries, keys, values, lengths, out_weight):
    tokens = queries.shape[0]
    with jax.named_scope("gather_keys_values"):
        lane = lax.broadcasted_iota(jnp.int32, (tokens, 2 * HD), 1)
        kv = jnp.where(
            lane < HD,
            jnp.pad(keys, ((0, 0), (0, HD))),
            jnp.pad(values, ((0, 0), (HD, 0))),
        )
        up2, down2 = ctx(kv, from_z(2)), ctx(kv, from_z(-2))
        up1, down1 = ctx(kv, from_z(1)), ctx(kv, from_z(-1))
        early = together([kv, up1, down1, up2, down2])
        right_a, left_a = ctx(early, from_x(1)), ctx(early, from_x(-1))
        up3, down3 = ctx(up2, from_z(1)), ctx(down2, from_z(-1))
        even = lax.axis_index("ctx") % 2 == 0
        over = ctx(jnp.where(even, up2, down2), OVER)
        later = together([up3, over, down3])
        right_b, left_b = ctx(later, from_x(1)), ctx(later, from_x(-1))
    with jax.named_scope("attend_own_row"):
        state = attend_to((0,), lengths, queries, [early, later])
    with jax.named_scope("gather_keys_values"):
        right_a, left_a = lax.optimization_barrier((right_a, left_a))
        far_a = ctx(right_a, from_x(1))
        right_b, left_b, state = lax.optimization_barrier((right_b, left_b, state))
        far_b = ctx(left_b, from_x(-1))
    with jax.named_scope("attend_next_rows"):
        state = attend_to((1, 3), lengths, queries, [right_a, right_b, left_a, left_b], state)
    with jax.named_scope("attend_far_row_and_project"):
        att, mine_2, other_2 = attend_to((2,), lengths, queries, [far_a, far_b], state, out_weight)
    with jax.named_scope("sum_over_heads"):

        def pair(a, b):
            return (a.astype(jnp.float32) + b.astype(jnp.float32)).astype(jnp.bfloat16)

        near = (0, 1, 3)
        theirs_2 = lax.ppermute(other_2, "tp", CORES)
        other = project_to(near, False, att, out_weight)
        theirs_2, other = lax.optimization_barrier((theirs_2, other))
        theirs = lax.ppermute(other, "tp", CORES)
        total = lax.ppermute(pair(mine_2, theirs_2), "tp", from_y(2)).astype(jnp.float32)
        mine = project_to(near, True, att, out_weight)
        for i, k in ((1, 1), (2, 3)):
            total += lax.ppermute(pair(mine[i], theirs[i]), "tp", from_y(-k)).astype(jnp.float32)
        total += mine[0].astype(jnp.float32) + theirs[0].astype(jnp.float32)
        return total.astype(jnp.bfloat16)


def solution(mesh):
    return jax.shard_map(
        on_device,
        mesh=mesh,
        in_specs=(P("ctx", "tp"), P("ctx", "tp"), P("ctx", "tp"), P(), P("tp", None)),
        out_specs=P("ctx", "tp"),
        check_vma=False,
    )
```

```python
import functools

import jax
import jax.numpy as jnp
from jax import lax
from jax.experimental import pallas as pl
from jax.experimental.pallas import tpu as pltpu
from jax.sharding import PartitionSpec as P

HD = 128
GROUP = 8
NX, NZ, NY = 4, 8, 4
HALF = 128
BLOCKS = 2 * NX * NZ
NEG = -1e30
SCALE2 = (HD ** -0.5) * 1.4426950408889634
OWN_Z, EARLY_Z, LATER_Z = (0,), (1, 7, 2, 6), (3, 4, 5)
VMEM = pl.BlockSpec(memory_space=pltpu.VMEM)
ANY = pl.BlockSpec(memory_space=pl.ANY)


def from_x(k):
    return [(((x + k) % NX) * NZ + z, x * NZ + z) for x in range(NX) for z in range(NZ)]


def from_z(k):
    return [(x * NZ + (z + k) % NZ, x * NZ + z) for x in range(NX) for z in range(NZ)]


def from_y(k):
    return [(((y + k) % NY) * 2 + c, y * 2 + c) for y in range(NY) for c in range(2)]


OVER = [(x * NZ + (z + (2 if z % 2 == 0 else -2)) % NZ, x * NZ + z) for x in range(NX) for z in range(NZ)]
CORES = [(y * 2 + c, y * 2 + 1 - c) for y in range(NY) for c in range(2)]


def ctx(a, perm):
    return lax.ppermute(a, "ctx", perm)


def lay_together(*refs):
    at = 0
    for piece in refs[:-1]:
        refs[-1][at : at + piece.shape[0], :] = piece[...]
        at += piece.shape[0]


def together(parts):
    rows = sum(p.shape[0] for p in parts)
    return pl.pallas_call(
        lay_together,
        out_shape=jax.ShapeDtypeStruct((rows, parts[0].shape[1]), parts[0].dtype),
        in_specs=[VMEM] * len(parts),
        out_specs=VMEM,
        compiler_params=pltpu.CompilerParams(vmem_limit_bytes=8 * 2**20),
    )(*parts)


def attend(jobs, first, last, *refs):
    refs = list(refs)
    take = lambda n: [refs.pop(0) for _ in range(n)]
    ends_hbm, q = take(2)
    w = take(1)[0] if last else None
    held = [(kx, [(take(1)[0], offsets) for offsets in pieces]) for kx, pieces in jobs]
    state = [] if first else take(2)
    att, mine_ref, other_ref = take(3) if last else (None, None, None)
    acc, top, lens, len_sem = take(4)
    me = lax.axis_index("ctx")
    mx, mz = me // NZ, me % NZ
    span = NZ * HALF

    len_copy = pltpu.make_async_copy(ends_hbm, lens, len_sem)
    len_copy.start()
    if first:
        acc[...] = jnp.zeros_like(acc)
        top[...] = jnp.full_like(top, NEG)
    else:
        acc[...] = state[0][...]
        top[...] = state[1][...]
    len_copy.wait()
    ends = [lens[i] for i in range(lens.shape[0])]

    def begins(p):
        start = jnp.zeros_like(p)
        for e in ends:
            start = jnp.maximum(start, jnp.where(p >= e, e, 0))
        return start

    def step(blocks, h, q0, late, k0, masked):
        n = len(blocks)
        k, v, kp = [], [], []
        for ref, i, kz in blocks:
            at = pl.ds(pl.multiple_of((2 * i + late) * HALF, HALF), HALF)
            k.append(ref[at, :HD])
            v.append(ref[at, HD:])
            z = (mz + kz) % NZ
            if masked:
                base = k0 + jnp.where(late == 0, z, NZ - 1 - z) * HALF
                kp.append(base + lax.broadcasted_iota(jnp.int32, (HALF, HALF), 1))
        k = jnp.concatenate(k, axis=0)
        ones = jnp.ones((n * HALF, HD), jnp.bfloat16)
        v = jnp.concatenate([jnp.concatenate(v, axis=0), ones], axis=1)
        if masked:
            kp = jnp.concatenate(kp, axis=1)
            qp = q0 + lax.broadcasted_iota(jnp.int32, (HALF, HD), 0)
            begin = jnp.tile(begins(qp), (1, n))
            ok = (kp <= jnp.tile(qp, (1, n))) & (kp >= begin)
        q_rows = pl.ds(pl.multiple_of(h * HALF, HALF), HALF)
        for g in range(GROUP):
            at = slice(g * HALF, (g + 1) * HALF)
            s = lax.dot_general(
                q[q_rows, g * HD : (g + 1) * HD],
                k,
                (((1,), (1,)), ((), ())),
                preferred_element_type=jnp.float32,
            )
            if masked:
                s = jnp.where(ok, s, NEG)
            old = top[h, at, :]
            new = jnp.maximum(old, jnp.max(s, axis=1, keepdims=True))
            p = jnp.exp2((s - jnp.tile(new, (1, n))) * SCALE2)
            o = jnp.dot(p.astype(jnp.bfloat16), v, preferred_element_type=jnp.float32)
            alpha = jnp.exp2((old - new) * SCALE2)
            acc[h, at, :] = acc[h, at, :] * jnp.tile(alpha, (1, 2)) + o
            top[h, at, :] = new

    for kx, pieces in held:
        x = (mx + kx) % NX
        blocks = [(ref, i, kz) for ref, offsets in pieces for i, kz in enumerate(offsets)]

        def one(n, carry, x=x, blocks=blocks):
            h, late = jnp.where(n == 0, 0, 1), jnp.where(n == 2, 1, 0)
            q0 = jnp.where(h == 0, me, BLOCKS - 1 - me) * HALF
            first_start, last_start = begins(q0), begins(q0 + HALF - 1)
            k0 = jnp.where(late == 0, x, 2 * NX - 1 - x) * span
            some = (k0 <= q0 + HALF - 1) & (k0 + span - 1 >= first_start)
            whole = (k0 >= last_start) & (k0 + span - 1 <= q0)
            pl.when(whole)(lambda: step(blocks, h, q0, late, k0, False))
            pl.when(some & jnp.logical_not(whole))(lambda: step(blocks, h, q0, late, k0, True))
            return carry

        lax.fori_loop(0, 3, one, 0)

    if last:
        for h in range(2):
            for g in range(GROUP):
                at = slice(g * HALF, (g + 1) * HALF)
                att[h * HALF : (h + 1) * HALF, g * HD : (g + 1) * HD] = (
                    acc[h, at, :HD] / acc[h, at, HD:]
                ).astype(jnp.bfloat16)
        for ref, same in ((other_ref, False), (mine_ref, True)):
            ref[...] = projected(att, w, 2, same)


def projected(att, w, k, same):
    tp = lax.axis_index("tp")
    width = w.shape[1] // (2 * NY)
    core = tp % 2 if same else 1 - tp % 2
    col = pl.multiple_of((((tp // 2 + k) % NY) * 2 + core) * width, width)
    return jnp.dot(
        att[...], w[:, pl.ds(col, width)], preferred_element_type=jnp.float32
    ).astype(jnp.bfloat16)


def project(ks, same, att, w, out):
    for i, k in enumerate(ks):
        out[i] = projected(att, w, k, same)


def project_to(ks, same, att, out_weight):
    shape = (len(ks), att.shape[0], out_weight.shape[1] // (2 * NY))
    return pl.pallas_call(
        functools.partial(project, ks, same),
        out_shape=jax.ShapeDtypeStruct(shape, jnp.bfloat16),
        in_specs=[VMEM] * 2,
        out_specs=VMEM,
        compiler_params=pltpu.CompilerParams(vmem_limit_bytes=14 * 2**20),
        cost_estimate=pl.CostEstimate(
            flops=270_000_000 * len(ks), bytes_accessed=2**20, transcendentals=0
        ),
    )(att, out_weight)


def attend_to(jobs, ends, queries, state=None, out_weight=None):
    first, last = state is None, out_weight is not None
    tokens = queries.shape[0]
    state_shape = [(2, GROUP * HALF, 2 * HD), (2, GROUP * HALF, HD)]
    outs = [jax.ShapeDtypeStruct(s, jnp.float32) for s in state_shape]
    operands = [ends, queries] + ([out_weight] if last else [])
    operands += [p for _, pieces in jobs for p, _ in pieces]
    operands += [] if first else list(state)
    scratch = [pltpu.SMEM(ends.shape, jnp.int32), pltpu.SemaphoreType.DMA]
    jobs = tuple((kx, tuple(offsets for _, offsets in pieces)) for kx, pieces in jobs)
    blocks = sum(len(offsets) for _, pieces in jobs for offsets in pieces)
    flops = 140_000_000 * blocks
    if last:
        width = out_weight.shape[1] // (2 * NY)
        scratch = [pltpu.VMEM(s, jnp.float32) for s in state_shape] + scratch
        outs = [jax.ShapeDtypeStruct(queries.shape, jnp.bfloat16)]
        outs += [jax.ShapeDtypeStruct((tokens, width), jnp.bfloat16)] * 2
        flops += 540_000_000
    return pl.pallas_call(
        functools.partial(attend, jobs, first, last),
        out_shape=outs,
        in_specs=[ANY] + [VMEM] * (len(operands) - 1),
        out_specs=[VMEM] * len(outs),
        scratch_shapes=scratch,
        compiler_params=pltpu.CompilerParams(vmem_limit_bytes=(22 if last else 14) * 2**20),
        cost_estimate=pl.CostEstimate(
            flops=flops, bytes_accessed=6 * 2**20, transcendentals=400_000 * blocks
        ),
    )(*operands)


def on_device(queries, keys, values, lengths, out_weight):
    tokens = queries.shape[0]
    with jax.named_scope("gather_keys_values"):
        lane = lax.broadcasted_iota(jnp.int32, (tokens, 2 * HD), 1)
        kv = jnp.where(
            lane < HD,
            jnp.pad(keys, ((0, 0), (0, HD))),
            jnp.pad(values, ((0, 0), (HD, 0))),
        )
        up2, down2 = ctx(kv, from_z(2)), ctx(kv, from_z(-2))
        up1, down1 = ctx(kv, from_z(1)), ctx(kv, from_z(-1))
        right_0, left_0 = ctx(kv, from_x(1)), ctx(kv, from_x(-1))
        early = together([up1, down1, up2, down2])
        before = jnp.tril(jnp.ones((lengths.shape[0],) * 2, bool))
        ends = jnp.sum(jnp.where(before, lengths[None, :], 0), axis=1)
        q = jnp.where(lax.axis_index("ctx") >= 0, queries, 0)
        early, right_0, left_0, q, ends = lax.optimization_barrier(
            (early, right_0, left_0, q, ends)
        )
        right_a, left_a = ctx(early, from_x(1)), ctx(early, from_x(-1))
        up3, down3 = ctx(up2, from_z(1)), ctx(down2, from_z(-1))
        even = lax.axis_index("ctx") % 2 == 0
        over = ctx(jnp.where(even, up2, down2), OVER)
        later = together([up3, over, down3])
    with jax.named_scope("attend_own_row_early"):
        jobs = [(0, [(kv, OWN_Z), (early, EARLY_Z)])]
        state = attend_to(jobs, ends, q)
    with jax.named_scope("gather_keys_values"):
        later, state = lax.optimization_barrier((later, state))
        right_b, left_b = ctx(later, from_x(1)), ctx(later, from_x(-1))
        right_a, left_a = lax.optimization_barrier((right_a, left_a))
        far_a = ctx(right_a, from_x(1))
        far_0 = ctx(left_0, from_x(-1))
    with jax.named_scope("attend_right_row_early"):
        jobs = [(0, [(later, LATER_Z)]), (1, [(right_0, OWN_Z), (right_a, EARLY_Z)])]
        state = attend_to(jobs, ends, q, state)
    with jax.named_scope("gather_keys_values"):
        right_b, left_b, state, far_0 = lax.optimization_barrier((right_b, left_b, state, far_0))
        far_b = ctx(left_b, from_x(-1))
    with jax.named_scope("attend_left_row"):
        jobs = [
            (3, [(left_0, OWN_Z), (left_a, EARLY_Z), (left_b, LATER_Z)]),
            (1, [(right_b, LATER_Z)]),
        ]
        state = attend_to(jobs, ends, q, state)
    with jax.named_scope("attend_far_row_and_project"):
        jobs = [(2, [(far_0, OWN_Z), (far_a, EARLY_Z), (far_b, LATER_Z)])]
        att, mine_2, other_2 = attend_to(jobs, ends, q, state, out_weight)
    with jax.named_scope("sum_over_heads"):

        def pair(a, b):
            return (a.astype(jnp.float32) + b.astype(jnp.float32)).astype(jnp.bfloat16)

        rest = (0, 1, 3)
        theirs_2 = lax.ppermute(other_2, "tp", CORES)
        other = project_to(rest, False, att, out_weight)
        theirs_2, other = lax.optimization_barrier((theirs_2, other))
        theirs = lax.ppermute(other, "tp", CORES)
        total = lax.ppermute(pair(mine_2, theirs_2), "tp", from_y(2)).astype(jnp.float32)
        mine = project_to(rest, True, att, out_weight)
        for i, k in ((1, 1), (2, 3)):
            total += lax.ppermute(pair(mine[i], theirs[i]), "tp", from_y(-k)).astype(jnp.float32)
        total += mine[0].astype(jnp.float32) + theirs[0].astype(jnp.float32)
        return total.astype(jnp.bfloat16)


def solution(mesh):
    return jax.shard_map(
        on_device,
        mesh=mesh,
        in_specs=(P("ctx", "tp"), P("ctx", "tp"), P("ctx", "tp"), P(), P("tp", None)),
        out_specs=P("ctx", "tp"),
        check_vma=False,
    )
```

```python
import functools

import jax
import jax.numpy as jnp
from jax import lax
from jax.experimental import pallas as pl
from jax.experimental.pallas import tpu as pltpu
from jax.sharding import PartitionSpec as P

HD = 128
GROUP = 8
NX, NZ, NY = 4, 8, 4
HALF = 128
BLOCKS = 2 * NX * NZ
NEG = -1e30
SCALE2 = (HD ** -0.5) * 1.4426950408889634
OWN_Z, EARLY_Z, LATER_Z = (0,), (1, 7, 2, 6), (3, 4, 5)
VMEM = pl.BlockSpec(memory_space=pltpu.VMEM)
ANY = pl.BlockSpec(memory_space=pl.ANY)


def from_x(k):
    return [(((x + k) % NX) * NZ + z, x * NZ + z) for x in range(NX) for z in range(NZ)]


def from_z(k):
    return [(x * NZ + (z + k) % NZ, x * NZ + z) for x in range(NX) for z in range(NZ)]


def from_y(k):
    return [(((y + k) % NY) * 2 + c, y * 2 + c) for y in range(NY) for c in range(2)]


OVER = [(x * NZ + (z + (2 if z % 2 == 0 else -2)) % NZ, x * NZ + z) for x in range(NX) for z in range(NZ)]
CORES = [(y * 2 + c, y * 2 + 1 - c) for y in range(NY) for c in range(2)]


def ctx(a, perm):
    return lax.ppermute(a, "ctx", perm)


def lay_together(*refs):
    at = 0
    for piece in refs[:-1]:
        refs[-1][at : at + piece.shape[0], :] = piece[...]
        at += piece.shape[0]


def together(parts):
    rows = sum(p.shape[0] for p in parts)
    return pl.pallas_call(
        lay_together,
        out_shape=jax.ShapeDtypeStruct((rows, parts[0].shape[1]), parts[0].dtype),
        in_specs=[VMEM] * len(parts),
        out_specs=VMEM,
        compiler_params=pltpu.CompilerParams(vmem_limit_bytes=8 * 2**20),
    )(*parts)


def attend(jobs, first, last, *refs):
    refs = list(refs)
    take = lambda n: [refs.pop(0) for _ in range(n)]
    ends_hbm, q = take(2)
    w = take(1)[0] if last else None
    held = [(kx, [(take(1)[0], offsets) for offsets in pieces]) for kx, pieces in jobs]
    state = [] if first else take(2)
    att, mine_ref, other_ref = take(3) if last else (None, None, None)
    acc, top, lens, len_sem = take(4)
    me = lax.axis_index("ctx")
    mx, mz = me // NZ, me % NZ
    span = NZ * HALF

    len_copy = pltpu.make_async_copy(ends_hbm, lens, len_sem)
    len_copy.start()
    if first:
        acc[...] = jnp.zeros_like(acc)
        top[...] = jnp.full_like(top, NEG)
    else:
        acc[...] = state[0][...]
        top[...] = state[1][...]
    len_copy.wait()
    ends = [lens[i] for i in range(lens.shape[0])]

    def begins(p):
        start = jnp.zeros_like(p)
        for e in ends:
            start = jnp.maximum(start, jnp.where(p >= e, e, 0))
        return start

    def step(blocks, h, q0, late, k0, masked):
        n = len(blocks)
        k, v, kp = [], [], []
        for ref, i, kz in blocks:
            at = pl.ds(pl.multiple_of((2 * i + late) * HALF, HALF), HALF)
            k.append(ref[at, :HD])
            v.append(ref[at, HD:])
            z = (mz + kz) % NZ
            if masked:
                base = k0 + jnp.where(late == 0, z, NZ - 1 - z) * HALF
                kp.append(base + lax.broadcasted_iota(jnp.int32, (HALF, HALF), 1))
        k = jnp.concatenate(k, axis=0)
        ones = jnp.ones((n * HALF, HD), jnp.bfloat16)
        v = jnp.concatenate([jnp.concatenate(v, axis=0), ones], axis=1)
        if masked:
            kp = jnp.concatenate(kp, axis=1)
            qp = q0 + lax.broadcasted_iota(jnp.int32, (HALF, HD), 0)
            begin = jnp.tile(begins(qp), (1, n))
            ok = (kp <= jnp.tile(qp, (1, n))) & (kp >= begin)
        q_rows = pl.ds(pl.multiple_of(h * HALF, HALF), HALF)
        for g in range(GROUP):
            at = slice(g * HALF, (g + 1) * HALF)
            s = lax.dot_general(
                q[q_rows, g * HD : (g + 1) * HD],
                k,
                (((1,), (1,)), ((), ())),
                preferred_element_type=jnp.float32,
            )
            if masked:
                s = jnp.where(ok, s, NEG)
            old = top[h, at, :]
            new = jnp.maximum(old, jnp.max(s, axis=1, keepdims=True))
            p = jnp.exp2((s - jnp.tile(new, (1, n))) * SCALE2)
            o = jnp.dot(p.astype(jnp.bfloat16), v, preferred_element_type=jnp.float32)
            alpha = jnp.exp2((old - new) * SCALE2)
            acc[h, at, :] = acc[h, at, :] * jnp.tile(alpha, (1, 2)) + o
            top[h, at, :] = new

    for kx, pieces in held:
        x = (mx + kx) % NX
        blocks = [(ref, i, kz) for ref, offsets in pieces for i, kz in enumerate(offsets)]

        def one(n, carry, x=x, blocks=blocks):
            h, late = jnp.where(n == 0, 0, 1), jnp.where(n == 2, 1, 0)
            q0 = jnp.where(h == 0, me, BLOCKS - 1 - me) * HALF
            first_start, last_start = begins(q0), begins(q0 + HALF - 1)
            k0 = jnp.where(late == 0, x, 2 * NX - 1 - x) * span
            some = (k0 <= q0 + HALF - 1) & (k0 + span - 1 >= first_start)
            whole = (k0 >= last_start) & (k0 + span - 1 <= q0)
            pl.when(whole)(lambda: step(blocks, h, q0, late, k0, False))
            pl.when(some & jnp.logical_not(whole))(lambda: step(blocks, h, q0, late, k0, True))
            return carry

        lax.fori_loop(0, 3, one, 0)

    if last:
        for h in range(2):
            for g in range(GROUP):
                at = slice(g * HALF, (g + 1) * HALF)
                att[h * HALF : (h + 1) * HALF, g * HD : (g + 1) * HD] = (
                    acc[h, at, :HD] / acc[h, at, HD:]
                ).astype(jnp.bfloat16)
        for ref, same in ((other_ref, False), (mine_ref, True)):
            ref[...] = projected(att, w, 2, same)


def projected(att, w, k, same):
    tp = lax.axis_index("tp")
    width = w.shape[1] // (2 * NY)
    core = tp % 2 if same else 1 - tp % 2
    col = pl.multiple_of((((tp // 2 + k) % NY) * 2 + core) * width, width)
    return jnp.dot(
        att[...], w[:, pl.ds(col, width)], preferred_element_type=jnp.float32
    ).astype(jnp.bfloat16)


def project(ks, same, att, w, out):
    for i, k in enumerate(ks):
        out[i] = projected(att, w, k, same)


def project_to(ks, same, att, out_weight):
    shape = (len(ks), att.shape[0], out_weight.shape[1] // (2 * NY))
    return pl.pallas_call(
        functools.partial(project, ks, same),
        out_shape=jax.ShapeDtypeStruct(shape, jnp.bfloat16),
        in_specs=[VMEM] * 2,
        out_specs=VMEM,
        compiler_params=pltpu.CompilerParams(vmem_limit_bytes=14 * 2**20),
        cost_estimate=pl.CostEstimate(
            flops=270_000_000 * len(ks), bytes_accessed=2**20, transcendentals=0
        ),
    )(att, out_weight)


def attend_to(jobs, ends, queries, state=None, out_weight=None):
    first, last = state is None, out_weight is not None
    tokens = queries.shape[0]
    state_shape = [(2, GROUP * HALF, 2 * HD), (2, GROUP * HALF, HD)]
    outs = [jax.ShapeDtypeStruct(s, jnp.float32) for s in state_shape]
    operands = [ends, queries] + ([out_weight] if last else [])
    operands += [p for _, pieces in jobs for p, _ in pieces]
    operands += [] if first else list(state)
    scratch = [pltpu.SMEM(ends.shape, jnp.int32), pltpu.SemaphoreType.DMA]
    jobs = tuple((kx, tuple(offsets for _, offsets in pieces)) for kx, pieces in jobs)
    blocks = sum(len(offsets) for _, pieces in jobs for offsets in pieces)
    flops = 140_000_000 * blocks
    if last:
        width = out_weight.shape[1] // (2 * NY)
        scratch = [pltpu.VMEM(s, jnp.float32) for s in state_shape] + scratch
        outs = [jax.ShapeDtypeStruct(queries.shape, jnp.bfloat16)]
        outs += [jax.ShapeDtypeStruct((tokens, width), jnp.bfloat16)] * 2
        flops += 540_000_000
    return pl.pallas_call(
        functools.partial(attend, jobs, first, last),
        out_shape=outs,
        in_specs=[ANY] + [VMEM] * (len(operands) - 1),
        out_specs=[VMEM] * len(outs),
        scratch_shapes=scratch,
        compiler_params=pltpu.CompilerParams(vmem_limit_bytes=(22 if last else 14) * 2**20),
        cost_estimate=pl.CostEstimate(
            flops=flops, bytes_accessed=6 * 2**20, transcendentals=400_000 * blocks
        ),
    )(*operands)


def on_device(queries, keys, values, lengths, out_weight):
    tokens = queries.shape[0]
    with jax.named_scope("gather_keys_values"):
        lane = lax.broadcasted_iota(jnp.int32, (tokens, 2 * HD), 1)
        kv = jnp.where(
            lane < HD,
            jnp.pad(keys, ((0, 0), (0, HD))),
            jnp.pad(values, ((0, 0), (HD, 0))),
        )
        up2, down2 = ctx(kv, from_z(2)), ctx(kv, from_z(-2))
        up1, down1 = ctx(kv, from_z(1)), ctx(kv, from_z(-1))
        right_0, left_0 = ctx(kv, from_x(1)), ctx(kv, from_x(-1))
        early = together([up1, down1, up2, down2])
        before = jnp.tril(jnp.ones((lengths.shape[0],) * 2, bool))
        ends = jnp.sum(jnp.where(before, lengths[None, :], 0), axis=1)
        q = jnp.where(lax.axis_index("ctx") >= 0, queries, 0)
        early, right_0, left_0, q, ends = lax.optimization_barrier(
            (early, right_0, left_0, q, ends)
        )
        right_a, left_a = ctx(early, from_x(1)), ctx(early, from_x(-1))
        up3, down3 = ctx(up2, from_z(1)), ctx(down2, from_z(-1))
        even = lax.axis_index("ctx") % 2 == 0
        over = ctx(jnp.where(even, up2, down2), OVER)
        later = together([up3, over, down3])
    with jax.named_scope("attend_own_row_early"):
        jobs = [(0, [(kv, OWN_Z), (early, EARLY_Z)])]
        state = attend_to(jobs, ends, q)
    with jax.named_scope("gather_keys_values"):
        later, state = lax.optimization_barrier((later, state))
        right_b, left_b = ctx(later, from_x(1)), ctx(later, from_x(-1))
        right_a, left_a = lax.optimization_barrier((right_a, left_a))
        far_a = ctx(right_a, from_x(1))
        far_0 = ctx(left_0, from_x(-1))
    with jax.named_scope("attend_right_row_early"):
        jobs = [(0, [(later, LATER_Z)]), (1, [(right_0, OWN_Z), (right_a, EARLY_Z)])]
        state = attend_to(jobs, ends, q, state)
    with jax.named_scope("gather_keys_values"):
        left_b, state, far_0 = lax.optimization_barrier((left_b, state, far_0))
        far_b = ctx(left_b, from_x(-1))
    with jax.named_scope("attend_left_row"):
        jobs = [
            (3, [(left_0, OWN_Z), (left_a, EARLY_Z), (left_b, LATER_Z)]),
            (1, [(right_b, LATER_Z)]),
        ]
        state = attend_to(jobs, ends, q, state)
    with jax.named_scope("attend_far_row_and_project"):
        jobs = [(2, [(far_0, OWN_Z), (far_a, EARLY_Z), (far_b, LATER_Z)])]
        att, mine_2, other_2 = attend_to(jobs, ends, q, state, out_weight)
    with jax.named_scope("sum_over_heads"):

        def pair(a, b):
            return (a.astype(jnp.float32) + b.astype(jnp.float32)).astype(jnp.bfloat16)

        rest = (0, 1, 3)
        theirs_2 = lax.ppermute(other_2, "tp", CORES)
        other = project_to(rest, False, att, out_weight)
        theirs_2, other = lax.optimization_barrier((theirs_2, other))
        theirs = lax.ppermute(other, "tp", CORES)
        total = lax.ppermute(pair(mine_2, theirs_2), "tp", from_y(2)).astype(jnp.float32)
        mine = project_to(rest, True, att, out_weight)
        for i, k in ((1, 1), (2, 3)):
            total += lax.ppermute(pair(mine[i], theirs[i]), "tp", from_y(-k)).astype(jnp.float32)
        total += mine[0].astype(jnp.float32) + theirs[0].astype(jnp.float32)
        return total.astype(jnp.bfloat16)


def solution(mesh):
    return jax.shard_map(
        on_device,
        mesh=mesh,
        in_specs=(P("ctx", "tp"), P("ctx", "tp"), P("ctx", "tp"), P(), P("tp", None)),
        out_specs=P("ctx", "tp"),
        check_vma=False,
    )
```
